32 devices in a mesh: rows: 8 (over z, y), cols: 4 (over x, core).
Axes of the slice: x: 2, y: 2, z: 4, core: 2. Of those that a mesh axis runs over, the one named last changes fastest.
Arguments:
- tile_blocks: bfloat16 [256, 8, 256, 256], P(('rows', 'cols')), may hold values from 0.049804688 to 1
- tile_cols: int32 [256, 8], P(('rows', 'cols')), may hold values from 0 to 255, as said below
- tile_count: int32 [256], P(('rows', 'cols')), may hold values from 1 to 8
- start_mass: float32 [65536], P(('rows', 'cols')), may hold values from 0.5 to 64
- probe_block: bfloat16 [32, 65536], P(None, ('rows', 'cols')), may hold values from -6 to 6
Outputs:
- basis: float32 [32, 65536], P(None, ('rows', 'cols'))
The draws below stay inside these ranges and needn't reach their ends.
Inputs may be any that keep to these rules, and one draw needn't show every extreme that they name: `tile_cols`: slot 0 names the block row itself; every other slot names a block within 8 blocks of its row, cyclically over 256.
All inputs are finite; a program needn't handle non-finite values.
Results may differ from the reference program's by a relative error of at most 0.00035.
The reference program's roundings to bfloat16 on the way count: a program that leaves them out, or rounds other values in their place, can miss the bound.
Values may be sent and summed in bfloat16 or wider, within the bound.
A program may use at most 64 MiB of HBM per device.

```python
import math
import jax
import jax.numpy as jnp
from jax import lax

TILE = 256
K = 8
COLS = 32
BR_DEV = 8
POWER = 4
BLOCKS = 256
ZONES = 65536


def draw_tile_cols(key, part):
    key = jax.random.fold_in(key, 7)
    offsets = jax.random.randint(key, (BLOCKS, K), -BR_DEV, BR_DEV + 1)
    slot_index = jnp.arange(K)[None, :]
    offsets = jnp.where(slot_index == 0, 0, offsets)
    base_rows = jnp.arange(BLOCKS)[:, None]
    return ((base_rows + offsets) % BLOCKS).astype(jnp.int32)


def rising_mass(rough, factor):
    place = jnp.arange(ZONES).astype(jnp.float32) / ZONES
    return (jnp.exp(jnp.log(factor) * place) * rough).astype(jnp.float32)


def draw_start_mass(key, part):
    key = jax.random.fold_in(key, 11)
    rough = jnp.exp(jax.random.uniform(key, (ZONES,), jnp.float32, jnp.log(0.5), jnp.log(2.0)))
    return rising_mass(rough, 8.0)


def set_ends(values, key, least, high):
    longest = values.shape.index(max(values.shape))
    spots = []
    for shift in (0, 1):
        where = [jax.random.randint(jax.random.fold_in(key, axis), (), 0, length) for axis, length in enumerate(values.shape)]
        where[longest] = (where[longest] + shift) % values.shape[longest]
        spots.append(tuple(where))
    return values.at[spots[0]].set(least).at[spots[1]].set(high)


def level_of(own_key, dims, split, least, largest):
    gain, own = 1.0, jax.random.fold_in(own_key, 6)
    for position, blocks in split:
        heights = jnp.exp(jax.random.uniform(jax.random.fold_in(own, position), (blocks,), jnp.float32, least / len(split), largest / len(split)))
        gain = gain * jnp.repeat(heights, dims[position] // blocks).reshape([-1 if axis == position else 1 for axis in range(len(dims))])
    return gain


def gaussian(own_key, extent, width, reach, shards=(), held_as=jnp.bfloat16):
    values = width * jax.random.normal(own_key, extent, jnp.float32)
    if shards:
        values = values * level_of(own_key, extent, shards, -0.22, 0.18)
    return jnp.clip(values, -reach, reach).astype(held_as)


def setup_inputs(seed: int = 0) -> dict:
    streams_of = jax.random.split(jax.random.key(seed), 6)
    return {
        "tile_blocks": jnp.clip(0.049804688 + 0.9501953 * jax.random.uniform(streams_of[0], (BLOCKS, K, TILE, TILE), jnp.float32) ** level_of(streams_of[0], (BLOCKS, K, TILE, TILE), ((0, 32),), -0.2, 0.2), 0.049804688, 1.0).astype(jnp.bfloat16),
        "tile_cols": draw_tile_cols(jax.random.fold_in(streams_of[5], 71), 0),
        "tile_count": set_ends(jax.random.randint(streams_of[2], (BLOCKS,), 1, K + 1), jax.random.fold_in(streams_of[2], 1), 1, K).astype(jnp.int32),
        "start_mass": draw_start_mass(jax.random.fold_in(streams_of[5], 71), 0),
        "probe_block": gaussian(streams_of[4], (COLS, ZONES), 1.0, 6.0, ((1, 32),)),
    }


def reference(tile_blocks, tile_cols, tile_count, start_mass, probe_block):
    highest = lax.Precision.HIGHEST
    live_slots = (jnp.arange(K)[None, :] < tile_count[:, None]).astype(jnp.float32)
    grouped = tile_blocks.reshape(BLOCKS // BR_DEV, BR_DEV, K, TILE, TILE)
    col_groups = tile_cols.reshape(BLOCKS // BR_DEV, BR_DEV, K)
    mask_groups = live_slots.reshape(BLOCKS // BR_DEV, BR_DEV, K)

    def row_part(group_tiles):
        return lax.optimization_barrier(jnp.sum(group_tiles.astype(jnp.float32), axis=3))
    partial_rows = lax.map(row_part, grouped).reshape(BLOCKS, K, TILE)
    row_sum = lax.optimization_barrier(jnp.sum(partial_rows * live_slots[:, :, None], axis=1))
    row_inverse = 1.0 / row_sum

    def transposed(weighted):
        chans = weighted.shape[0]
        w_groups = weighted.reshape(chans, BLOCKS // BR_DEV, BR_DEV, TILE).transpose(1, 0, 2, 3)

        def add_group(carried, items):
            group_tiles, group_w, group_cols, group_mask = items
            contrib = jnp.einsum('bkij,cbi->cbkj', group_tiles.astype(jnp.float32), group_w.astype(jnp.float32), precision=highest)
            contrib = contrib * group_mask[None, :, :, None]
            return (carried.at[:, group_cols.reshape(-1)].add(contrib.reshape(chans, BR_DEV * K, TILE)), None)
        result, ignored = lax.scan(add_group, jnp.zeros((chans, BLOCKS, TILE), jnp.float32), (grouped, w_groups, col_groups, mask_groups))
        return result

    def forward(operand):
        chans = operand.shape[0]

        def one_group(items):
            group_tiles, group_cols, group_mask = items
            gathered = operand[:, group_cols].astype(jnp.float32) * group_mask[None, :, :, None]
            return jnp.einsum('bkij,cbkj->cbi', group_tiles.astype(jnp.float32), gathered, precision=highest)
        result = lax.map(one_group, (grouped, col_groups, mask_groups))
        return result.transpose(1, 0, 2, 3).reshape(chans, BLOCKS, TILE)
    zone_root = math.sqrt(ZONES)
    stationary = start_mass.reshape(BLOCKS, TILE)
    for power_step in range(POWER):
        weighted = (stationary * row_inverse).astype(jnp.bfloat16)
        arrived = transposed(weighted[None])[0]
        raw_mass = 0.85 * arrived + 0.15
        stationary = raw_mass * zone_root / jnp.sqrt(jnp.sum(raw_mass * raw_mass))
    root_mass = jnp.sqrt(stationary)
    probe_rows = probe_block.reshape(COLS, BLOCKS, TILE).astype(jnp.float32)
    scaled_probe = (probe_rows / root_mass[None]).astype(jnp.bfloat16)
    forward_term = forward(scaled_probe) * (root_mass * row_inverse)[None]
    pushed = (probe_rows * (root_mass * row_inverse)[None]).astype(jnp.bfloat16)
    transposed_term = transposed(pushed) / root_mass[None]
    embedded = (0.5 * (forward_term + transposed_term)).reshape(COLS, ZONES)
    gram_matrix = jnp.dot(embedded, embedded.T, precision=highest)
    lower_factor = jnp.linalg.cholesky(gram_matrix)
    return jax.scipy.linalg.solve_triangular(lower_factor, embedded, lower=True)
```

```python
import functools
import math

import jax
import jax.numpy as jnp
from jax import lax
from jax.experimental import pallas as pl
from jax.experimental.pallas import tpu as pltpu
from jax.sharding import PartitionSpec as P

POWER = 4
MESH = pl.DeviceIdType.MESH
F32 = jnp.float32
BF16 = jnp.bfloat16


def split3(value):
    high = value.astype(BF16)
    rest = value - high.astype(F32)
    middle = rest.astype(BF16)
    low = (rest - middle.astype(F32)).astype(BF16)
    return high, middle, low


def kernel(
    row_axis, col_axis, blocks, slots, tile, chans,
    cols_ref, count_ref, tiles_hbm, mass_ref, probe_ref, out_ref,
    tiles, place, window, landed, raw_halo, sums, probe_halo, scaled, products,
    low, mid, up, from_left, from_right, emb_parts, embedded, grams,
    load_sem, sum_send, sum_recv, win_send, win_recv, halo_send, halo_recv,
    probe_send, probe_recv, part_send, part_recv, gram_send, gram_recv,
):
    devices = row_axis * col_axis
    me = lax.axis_index("rows") * col_axis + lax.axis_index("cols")
    right = lax.rem(me + 1, devices)
    left = lax.rem(me + devices - 1, devices)
    total_blocks = devices * blocks
    pairs = blocks * slots
    span = 4 * blocks

    def place_of(device):
        return (device // col_axis, lax.rem(device, col_axis))

    def remote(src, dst, send, recv, device):
        return pltpu.make_async_remote_copy(
            src_ref=src, dst_ref=dst, send_sem=send, recv_sem=recv,
            device_id=place_of(device), device_id_type=MESH,
        )

    loads = [
        pltpu.make_async_copy(tiles_hbm.at[b], tiles.at[b], load_sem.at[b]) for b in range(blocks)
    ]
    for load in loads:
        load.start()

    barrier = pltpu.get_barrier_semaphore()

    def greet(step, carry):
        other = lax.rem(me + step, devices)
        pl.semaphore_signal(barrier, inc=1, device_id=place_of(other), device_id_type=MESH)
        return carry

    lax.fori_loop(1, devices, greet, 0)

    first = me * blocks
    spot = []
    alive = []
    for b in range(blocks):
        for k in range(slots):
            at = cols_ref[b, k] - first + blocks
            at = jnp.where(at < 0, at + total_blocks, at)
            at = jnp.where(at >= total_blocks, at - total_blocks, at)
            live = k < count_ref[b]
            spot.append(jnp.where(live, at, 3 * blocks))
            alive.append(live)
    rows_iota = lax.broadcasted_iota(jnp.int32, (span, 128), 0)
    lane3 = lax.rem(lax.broadcasted_iota(jnp.int32, (8, 3 * pairs), 1), pairs)
    spot_row = jnp.zeros((8, 3 * pairs), jnp.int32)
    for s in range(pairs):
        hit = jnp.where(rows_iota == spot[s], 1.0, 0.0)
        hit = jnp.where(rows_iota < 3 * blocks, hit, 0.0).astype(BF16)
        k = s % slots
        for part in range(tile // 128):
            place[s // slots, :, k * tile + part * 128 : k * tile + (part + 1) * 128] = hit
        spot_row = jnp.where(lane3 == s, spot[s], spot_row)
    rows3 = lax.broadcasted_iota(jnp.int32, (span, 3 * pairs), 0)
    place3 = jnp.where(rows3 == spot_row[0:1], 1.0, 0.0).astype(BF16)
    scaled[3 * blocks] = jnp.zeros((chans, tile), BF16)

    pl.semaphore_wait(barrier, devices - 1)

    probe_right = remote(probe_ref, probe_halo.at[0], probe_send.at[0], probe_recv.at[0], right)
    probe_left = remote(probe_ref, probe_halo.at[1], probe_send.at[1], probe_recv.at[1], left)
    probe_right.start()
    probe_left.start()

    contract_last = (((1,), (1,)), ((), ()))
    sum_rows = lax.broadcasted_iota(jnp.int32, (16, tile), 0)
    row_sum = jnp.zeros((16, tile), F32)
    for b in range(blocks):
        loads[b].wait()
        for k in range(slots):
            weight = jnp.where(alive[b * slots + k], 1.0, 0.0)
            chosen = jnp.where(sum_rows == b, weight, 0.0).astype(BF16)
            row_sum += lax.dot_general(
                chosen, tiles[b, k], contract_last, preferred_element_type=F32
            )
    row_inverse = 1.0 / row_sum[:blocks]

    def spread(step, stationary):
        weighted = (stationary * row_inverse).astype(BF16).astype(F32)
        total = jnp.zeros((span, tile), F32)
        for b in range(blocks):
            row = jnp.broadcast_to(weighted[b : b + 1], (span, tile)).astype(BF16)
            lhs = place[b] * jnp.concatenate([row] * slots, axis=1)
            total += jnp.dot(
                lhs, tiles[b].reshape(slots * tile, tile), preferred_element_type=F32
            )
        window[step] = total[: 3 * blocks]
        to_left = remote(
            window.at[step, pl.ds(0, blocks)], landed.at[step, 1],
            win_send.at[step, 0], win_recv.at[step, 1], left,
        )
        to_right = remote(
            window.at[step, pl.ds(2 * blocks, blocks)], landed.at[step, 0],
            win_send.at[step, 1], win_recv.at[step, 0], right,
        )
        to_left.start()
        to_right.start()
        to_left.wait_recv()
        to_right.wait_recv()
        arrived = total[blocks : 2 * blocks] + landed[step, 0] + landed[step, 1]
        return 0.85 * arrived + 0.15

    def push_all(buffer, send, recv):
        def push(offset, carry):
            other = lax.rem(me + offset, devices)
            remote(buffer.at[me], buffer.at[me], send, recv, other).start()
            return carry

        lax.fori_loop(1, devices, push, 0)

    def wait_all(buffer, sem):
        view = buffer.at[pl.ds(0, devices - 1)]
        pltpu.make_async_copy(view, view, sem).wait()

    def begin_norm(step, raw):
        square = raw * raw
        folded = square[:, :128]
        for part in range(1, tile // 128):
            folded += square[:, part * 128 : (part + 1) * 128]
        sums[step, me] = folded
        push_all(sums.at[step], sum_send.at[step], sum_recv.at[step])

    def end_norm(step):
        wait_all(sums.at[step], sum_recv.at[step])
        total = jnp.sum(sums[step], axis=0)
        total = jnp.sum(jnp.sum(total, axis=0, keepdims=True), axis=1, keepdims=True)
        return math.sqrt(total_blocks * tile) / jnp.sqrt(total)

    def power(step, stationary):
        raw = spread(step, stationary)
        begin_norm(step, raw)
        return raw * end_norm(step)

    stationary = lax.fori_loop(0, POWER - 1, power, mass_ref[...])
    raw = spread(POWER - 1, stationary)
    raw_halo[1] = raw
    raw_right = remote(raw_halo.at[1], raw_halo.at[0], halo_send.at[0], halo_recv.at[0], right)
    raw_left = remote(raw_halo.at[1], raw_halo.at[2], halo_send.at[1], halo_recv.at[1], left)
    raw_right.start()
    raw_left.start()
    begin_norm(POWER - 1, raw)
    norm = end_norm(POWER - 1)
    root = jnp.sqrt(raw * norm)
    root_inverse = 1.0 / root
    gain = root * row_inverse

    halves = tile // 128
    for b in range(blocks):
        probe = probe_ref[:, b * tile : (b + 1) * tile].astype(F32)
        pushed = (probe * gain[b : b + 1]).astype(BF16)
        for k in range(slots):
            product = jnp.dot(pushed, tiles[b, k], preferred_element_type=F32)
            at = (b * slots + k) * chans
            for h in range(halves):
                products[h, at : at + chans, :] = product[:, h * 128 : (h + 1) * 128]
    for c in range(chans):
        for h in range(halves):
            slab = products.at[h][pl.ds(c, pairs, stride=chans), :]
            parts = jnp.concatenate(split3(slab), axis=0)
            placed = jnp.dot(place3, parts, preferred_element_type=F32)
            low[h, c * blocks : (c + 1) * blocks, :] = placed[:blocks]
            mid[h, c * blocks : (c + 1) * blocks, :] = placed[blocks : 2 * blocks]
            up[h, c * blocks : (c + 1) * blocks, :] = placed[2 * blocks : 3 * blocks]
    part_left = remote(low, from_right, part_send.at[0], part_recv.at[0], left)
    part_right = remote(up, from_left, part_send.at[1], part_recv.at[1], right)
    part_left.start()
    part_right.start()

    probe_right.wait_recv()
    probe_left.wait_recv()
    raw_right.wait_recv()
    raw_left.wait_recv()
    for side, part in ((0, 0), (1, None), (2, 1)):
        if part is None:
            inverse = root_inverse
        else:
            inverse = 1.0 / jnp.sqrt(raw_halo[side] * norm)
        for b in range(blocks):
            lanes = slice(b * tile, (b + 1) * tile)
            probe = probe_ref[:, lanes] if part is None else probe_halo[part, :, lanes]
            scaled[side * blocks + b] = (probe.astype(F32) * inverse[b : b + 1]).astype(BF16)
    for b in range(blocks):
        forward = jnp.zeros((chans, tile), F32)
        for k in range(slots):
            forward += lax.dot_general(
                scaled[spot[b * slots + k]], tiles[b, k], contract_last,
                preferred_element_type=F32,
            )
        embedded[:, b * tile : (b + 1) * tile] = forward * gain[b : b + 1]

    part_left.wait_recv()
    part_right.wait_recv()
    for b in range(blocks):
        for h in range(halves):
            lanes = slice(b * tile + h * 128, b * tile + (h + 1) * 128)
            rows = pl.ds(b, chans, stride=blocks)
            arrived = mid.at[h][rows, :] + from_left.at[h][rows, :] + from_right.at[h][rows, :]
            back = arrived * root_inverse[b : b + 1, h * 128 : (h + 1) * 128]
            value = 0.5 * (embedded[:, lanes] + back)
            for index, piece in enumerate(split3(value)):
                emb_parts[index * chans : (index + 1) * chans, lanes] = piece

    cross = lax.dot_general(
        emb_parts[...], emb_parts[...], contract_last, preferred_element_type=F32
    )
    gram = jnp.zeros((chans, chans), F32)
    for i, j in ((2, 2), (1, 2), (2, 1), (0, 2), (2, 0), (1, 1), (0, 1), (1, 0), (0, 0)):
        gram += cross[i * chans : (i + 1) * chans, j * chans : (j + 1) * chans]
    groups = chans // 8
    grams[me] = jnp.concatenate([gram[g * 8 : (g + 1) * 8] for g in range(groups)], axis=1)
    push_all(grams, gram_send, gram_recv)
    wait_all(grams, gram_recv)
    packed = jnp.sum(grams[...], axis=0)
    gram = jnp.concatenate(
        [packed[:, g * chans : (g + 1) * chans] for g in range(groups)], axis=0
    )

    row_id = lax.broadcasted_iota(jnp.int32, (chans, chans), 0)
    col_id = lax.broadcasted_iota(jnp.int32, (chans, chans), 1)
    work = jnp.concatenate([gram, jnp.where(row_id == col_id, 1.0, 0.0)], axis=1)
    row_wide = lax.broadcasted_iota(jnp.int32, (chans, 2 * chans), 0)
    pivots = jnp.ones((chans, 2 * chans), F32)
    for k in range(chans):
        pivot = work[k : k + 1, k : k + 1]
        pivots = jnp.where(row_wide == k, pivot, pivots)
        scaled_row = work[k : k + 1] * (1.0 / pivot)
        below = jnp.where(row_wide > k, work[:, k : k + 1], 0.0)
        work = work - below * scaled_row
    inverse = (work * lax.rsqrt(pivots))[:, chans:]
    ih, im, il = split3(inverse)
    lhs = jnp.concatenate([ih, im, il, ih, im, ih], axis=1)
    eh = emb_parts[:chans]
    em = emb_parts[chans : 2 * chans]
    el = emb_parts[2 * chans :]
    rhs = jnp.concatenate([eh, eh, eh, em, em, el], axis=0)
    out_ref[...] = jnp.dot(lhs, rhs, preferred_element_type=F32)

    probe_right.wait_send()
    probe_left.wait_send()
    raw_right.wait_send()
    raw_left.wait_send()
    part_left.wait_send()
    part_right.wait_send()

    def drain(step, carry):
        wait_all(sums.at[step], sum_send.at[step])
        for side, at in ((0, 0), (1, 2 * blocks)):
            view = window.at[step, pl.ds(at, blocks)]
            pltpu.make_async_copy(view, view, win_send.at[step, side]).wait()
        return carry

    lax.fori_loop(0, POWER, drain, 0)
    wait_all(grams, gram_send)


def per_device(row_axis, col_axis, tile_blocks, tile_cols, tile_count, start_mass, probe_block):
    blocks, slots, tile = tile_blocks.shape[:3]
    chans = probe_block.shape[0]
    devices = row_axis * col_axis
    zones = blocks * tile
    halves = tile // 128
    vmem = pl.BlockSpec(memory_space=pltpu.VMEM)
    smem = pl.BlockSpec(memory_space=pltpu.SMEM)
    dma = pltpu.SemaphoreType.DMA
    part = pltpu.VMEM((halves, chans * blocks, 128), F32)
    return pl.pallas_call(
        functools.partial(kernel, row_axis, col_axis, blocks, slots, tile, chans),
        out_shape=jax.ShapeDtypeStruct((chans, zones), F32),
        in_specs=[smem, smem, pl.BlockSpec(memory_space=pl.ANY), vmem, vmem],
        out_specs=vmem,
        scratch_shapes=[
            pltpu.VMEM((blocks, slots, tile, tile), BF16),
            pltpu.VMEM((blocks, 4 * blocks, slots * tile), BF16),
            pltpu.VMEM((POWER, 3 * blocks, tile), F32),
            pltpu.VMEM((POWER, 2, blocks, tile), F32),
            pltpu.VMEM((3, blocks, tile), F32),
            pltpu.VMEM((POWER, devices, 8, 128), F32),
            pltpu.VMEM((2, chans, zones), BF16),
            pltpu.VMEM((3 * blocks + 1, chans, tile), BF16),
            pltpu.VMEM((halves, blocks * slots * chans, 128), F32),
            part, part, part, part, part,
            pltpu.VMEM((3 * chans, zones), BF16),
            pltpu.VMEM((chans, zones), F32),
            pltpu.VMEM((devices, 8, 128), F32),
            dma((blocks,)),
            dma((POWER,)), dma((POWER,)),
            dma((POWER, 2)), dma((POWER, 2)),
            dma((2,)), dma((2,)),
            dma((2,)), dma((2,)),
            dma((2,)), dma((2,)),
            dma, dma,
        ],
        compiler_params=pltpu.CompilerParams(
            collective_id=0, has_side_effects=True, vmem_limit_bytes=48 * 1024 * 1024
        ),
        name="embed",
    )(tile_cols, tile_count, tile_blocks, start_mass.reshape(blocks, tile), probe_block)


def solution(mesh):
    sizes = dict(mesh.shape)
    return jax.shard_map(
        functools.partial(per_device, sizes["rows"], sizes["cols"]),
        mesh=mesh,
        in_specs=(
            P(("rows", "cols"), None, None, None),
            P(("rows", "cols"), None),
            P(("rows", "cols")),
            P(("rows", "cols")),
            P(None, ("rows", "cols")),
        ),
        out_specs=P(None, ("rows", "cols")),
        check_vma=False,
    )
```

```python
import functools
import math

import jax
import jax.numpy as jnp
from jax import lax
from jax.experimental import pallas as pl
from jax.experimental.pallas import tpu as pltpu
from jax.sharding import PartitionSpec as P

POWER = 4
MESH = pl.DeviceIdType.MESH
F32 = jnp.float32
BF16 = jnp.bfloat16


def split3(value):
    high = value.astype(BF16)
    rest = value - high.astype(F32)
    middle = rest.astype(BF16)
    low = (rest - middle.astype(F32)).astype(BF16)
    return high, middle, low


def kernel(
    row_axis, col_axis, group, blocks, slots, tile, chans,
    cols_hbm, count_hbm, tiles_hbm, mass_hbm, probe_hbm, out_ref,
    cols_ref, count_ref, mass_ref, probe_ref,
    tiles, place, window, landed, raw_halo, near_sums, far_sums, probe_halo, scaled, products,
    low, mid, up, from_left, from_right, emb_parts, embedded, near_grams, far_grams,
    small_sem, load_sem, near_send, near_recv, far_send, far_recv,
    win_send, win_recv, halo_send, halo_recv,
    probe_send, probe_recv, part_send, part_recv, gram_send, gram_recv,
):
    devices = row_axis * col_axis
    me = lax.axis_index("rows") * col_axis + lax.axis_index("cols")
    right = lax.rem(me + 1, devices)
    left = lax.rem(me + devices - 1, devices)
    total_blocks = devices * blocks
    pairs = blocks * slots
    span = 4 * blocks
    groups = devices // group
    my_group = me // group
    my_member = lax.rem(me, group)

    def place_of(device):
        return (device // col_axis, lax.rem(device, col_axis))

    def remote(src, dst, send, recv, device):
        return pltpu.make_async_remote_copy(
            src_ref=src, dst_ref=dst, send_sem=send, recv_sem=recv,
            device_id=place_of(device), device_id_type=MESH,
        )

    smalls = [
        pltpu.make_async_copy(src, dst, small_sem.at[i])
        for i, (src, dst) in enumerate(
            ((cols_hbm, cols_ref), (count_hbm, count_ref), (probe_hbm, probe_ref), (mass_hbm, mass_ref))
        )
    ]
    for small in smalls:
        small.start()
    loads = [
        pltpu.make_async_copy(tiles_hbm.at[b], tiles.at[b], load_sem.at[b]) for b in range(blocks)
    ]
    for load in loads:
        load.start()

    barrier = pltpu.get_barrier_semaphore()

    def near(offset):
        return my_group * group + lax.rem(my_member + offset, group)

    def far(offset):
        return lax.rem(my_group + offset, groups) * group + my_member

    def greet(other):
        pl.semaphore_signal(barrier, inc=1, device_id=place_of(other), device_id_type=MESH)

    def each(count, action):
        def body(offset, carry):
            action(offset)
            return carry

        lax.fori_loop(1, count, body, 0, unroll=count <= 8)

    greet(left)
    greet(right)
    each(group, lambda offset: greet(near(offset)))
    each(groups, lambda offset: greet(far(offset)))
    smalls[0].wait()
    smalls[1].wait()

    first = me * blocks
    spot = []
    alive = []
    for b in range(blocks):
        for k in range(slots):
            at = cols_ref[b, k] - first + blocks
            at = jnp.where(at < 0, at + total_blocks, at)
            at = jnp.where(at >= total_blocks, at - total_blocks, at)
            live = k < count_ref[b]
            spot.append(jnp.where(live, at, 3 * blocks))
            alive.append(live)
    rows_iota = lax.broadcasted_iota(jnp.int32, (span, 128), 0)
    lane3 = lax.rem(lax.broadcasted_iota(jnp.int32, (8, 3 * pairs), 1), pairs)
    spot_row = jnp.zeros((8, 3 * pairs), jnp.int32)
    for s in range(pairs):
        hit = jnp.where(rows_iota == spot[s], 1.0, 0.0)
        hit = jnp.where(rows_iota < 3 * blocks, hit, 0.0).astype(BF16)
        k = s % slots
        for part in range(tile // 128):
            place[s // slots, :, k * tile + part * 128 : k * tile + (part + 1) * 128] = hit
        spot_row = jnp.where(lane3 == s, spot[s], spot_row)
    rows3 = lax.broadcasted_iota(jnp.int32, (span, 3 * pairs), 0)
    place3 = jnp.where(rows3 == spot_row[0:1], 1.0, 0.0).astype(BF16)
    scaled[3 * blocks] = jnp.zeros((chans, tile), BF16)

    smalls[2].wait()
    pl.semaphore_wait(barrier, group + groups)

    probe_right = remote(probe_ref, probe_halo.at[0], probe_send.at[0], probe_recv.at[0], right)
    probe_left = remote(probe_ref, probe_halo.at[1], probe_send.at[1], probe_recv.at[1], left)
    probe_right.start()
    probe_left.start()

    contract_last = (((1,), (1,)), ((), ()))
    sum_rows = lax.broadcasted_iota(jnp.int32, (16, tile), 0)
    row_sum = jnp.zeros((16, tile), F32)
    for b in range(blocks):
        loads[b].wait()
        for k in range(slots):
            weight = jnp.where(alive[b * slots + k], 1.0, 0.0)
            chosen = jnp.where(sum_rows == b, weight, 0.0).astype(BF16)
            row_sum += lax.dot_general(
                chosen, tiles[b, k], contract_last, preferred_element_type=F32
            )
    row_inverse = 1.0 / row_sum[:blocks]

    def push_near(buffer, send, recv):
        each(
            group,
            lambda offset: remote(
                buffer.at[my_member], buffer.at[my_member], send, recv, near(offset)
            ).start(),
        )

    def push_far(buffer, send, recv):
        each(
            groups,
            lambda offset: remote(
                buffer.at[my_group], buffer.at[my_group], send, recv, far(offset)
            ).start(),
        )

    def wait_all(buffer, sem, count):
        view = buffer.at[pl.ds(0, count - 1)]
        pltpu.make_async_copy(view, view, sem).wait()

    def norm_near(step, raw):
        square = raw * raw
        folded = square[:, :128]
        for part in range(1, tile // 128):
            folded += square[:, part * 128 : (part + 1) * 128]
        near_sums[step, my_member] = jnp.sum(folded, axis=0, keepdims=True)
        push_near(near_sums.at[step], near_send.at[step], near_recv.at[step])

    def norm_far(step):
        wait_all(near_sums.at[step], near_recv.at[step], group)
        far_sums[step, my_group] = jnp.sum(near_sums[step], axis=0)
        push_far(far_sums.at[step], far_send.at[step], far_recv.at[step])

    def norm_end(step):
        wait_all(far_sums.at[step], far_recv.at[step], groups)
        total = jnp.sum(jnp.sum(far_sums[step], axis=0), axis=1, keepdims=True)
        return math.sqrt(total_blocks * tile) / jnp.sqrt(total)

    def spread(step, mass):
        weighted = (mass * row_inverse).astype(BF16).astype(F32)
        total = jnp.zeros((span, tile), F32)
        for b in range(blocks):
            row = jnp.broadcast_to(weighted[b : b + 1], (span, tile)).astype(BF16)
            lhs = place[b] * jnp.concatenate([row] * slots, axis=1)
            total += jnp.dot(
                lhs, tiles[b].reshape(slots * tile, tile), preferred_element_type=F32
            )
        window[step] = total[: 3 * blocks]
        to_left = remote(
            window.at[step, pl.ds(0, blocks)], landed.at[step, 1],
            win_send.at[step, 0], win_recv.at[step, 1], left,
        )
        to_right = remote(
            window.at[step, pl.ds(2 * blocks, blocks)], landed.at[step, 0],
            win_send.at[step, 1], win_recv.at[step, 0], right,
        )
        to_left.start()
        to_right.start()
        to_left.wait_recv()
        to_right.wait_recv()
        arrived = total[blocks : 2 * blocks] + landed[step, 0] + landed[step, 1]
        return 0.85 * arrived + 0.15

    smalls[3].wait()
    start = jnp.concatenate(
        [mass_ref[pl.ds(b * tile, tile)].reshape(1, tile) for b in range(blocks)], axis=0
    )

    def power(step, mass):
        raw = spread(step, mass)
        norm_near(step, raw)
        norm_far(step)
        return raw * norm_end(step)

    raw = spread(POWER - 1, lax.fori_loop(0, POWER - 1, power, start))
    norm_near(POWER - 1, raw)
    raw_halo[1] = raw
    raw_right = remote(raw_halo.at[1], raw_halo.at[0], halo_send.at[0], halo_recv.at[0], right)
    raw_left = remote(raw_halo.at[1], raw_halo.at[2], halo_send.at[1], halo_recv.at[1], left)
    raw_right.start()
    raw_left.start()
    norm_far(POWER - 1)
    norm = norm_end(POWER - 1)
    root = jnp.sqrt(raw * norm)
    root_inverse = 1.0 / root
    gain = root * row_inverse

    halves = tile // 128
    for b in range(blocks):
        probe = probe_ref[:, b * tile : (b + 1) * tile].astype(F32)
        pushed = (probe * gain[b : b + 1]).astype(BF16)
        for k in range(slots):
            product = jnp.dot(pushed, tiles[b, k], preferred_element_type=F32)
            at = (b * slots + k) * chans
            for h in range(halves):
                products[h, at : at + chans, :] = product[:, h * 128 : (h + 1) * 128]
    part_copies = []
    for h in range(halves):
        for c in range(chans):
            slab = products.at[h][pl.ds(c, pairs, stride=chans), :]
            parts = jnp.concatenate(split3(slab), axis=0)
            placed = jnp.dot(place3, parts, preferred_element_type=F32)
            low[h, c * blocks : (c + 1) * blocks, :] = placed[:blocks]
            mid[h, c * blocks : (c + 1) * blocks, :] = placed[blocks : 2 * blocks]
            up[h, c * blocks : (c + 1) * blocks, :] = placed[2 * blocks : 3 * blocks]
        to_left = remote(low.at[h], from_right.at[h], part_send.at[0, h], part_recv.at[0, h], left)
        to_right = remote(up.at[h], from_left.at[h], part_send.at[1, h], part_recv.at[1, h], right)
        to_left.start()
        to_right.start()
        part_copies += [to_left, to_right]

    probe_right.wait_recv()
    probe_left.wait_recv()
    raw_right.wait_recv()
    raw_left.wait_recv()
    for side, part in ((0, 0), (1, None), (2, 1)):
        if part is None:
            inverse = root_inverse
        else:
            inverse = 1.0 / jnp.sqrt(raw_halo[side] * norm)
        for b in range(blocks):
            lanes = slice(b * tile, (b + 1) * tile)
            probe = probe_ref[:, lanes] if part is None else probe_halo[part, :, lanes]
            scaled[side * blocks + b] = (probe.astype(F32) * inverse[b : b + 1]).astype(BF16)
    for b in range(blocks):
        forward = jnp.zeros((chans, tile), F32)
        for k in range(slots):
            forward += lax.dot_general(
                scaled[spot[b * slots + k]], tiles[b, k], contract_last,
                preferred_element_type=F32,
            )
        embedded[:, b * tile : (b + 1) * tile] = forward * gain[b : b + 1]

    for copy in part_copies:
        copy.wait_recv()
    for b in range(blocks):
        for h in range(halves):
            lanes = slice(b * tile + h * 128, b * tile + (h + 1) * 128)
            rows = pl.ds(b, chans, stride=blocks)
            arrived = mid.at[h][rows, :] + from_left.at[h][rows, :] + from_right.at[h][rows, :]
            back = arrived * root_inverse[b : b + 1, h * 128 : (h + 1) * 128]
            value = 0.5 * (embedded[:, lanes] + back)
            for index, piece in enumerate(split3(value)):
                emb_parts[index * chans : (index + 1) * chans, lanes] = piece

    cross = lax.dot_general(
        emb_parts[...], emb_parts[...], contract_last, preferred_element_type=F32
    )
    gram = jnp.zeros((chans, chans), F32)
    for i, j in ((2, 2), (1, 2), (2, 1), (0, 2), (2, 0), (1, 1), (0, 1), (1, 0), (0, 0)):
        gram += cross[i * chans : (i + 1) * chans, j * chans : (j + 1) * chans]
    quarters = chans // 8
    near_grams[my_member] = jnp.concatenate(
        [gram[q * 8 : (q + 1) * 8] for q in range(quarters)], axis=1
    )
    push_near(near_grams, gram_send.at[0], gram_recv.at[0])
    wait_all(near_grams, gram_recv.at[0], group)
    far_grams[my_group] = jnp.sum(near_grams[...], axis=0)
    push_far(far_grams, gram_send.at[1], gram_recv.at[1])
    wait_all(far_grams, gram_recv.at[1], groups)
    packed = jnp.sum(far_grams[...], axis=0)
    gram = jnp.concatenate(
        [packed[:, q * chans : (q + 1) * chans] for q in range(quarters)], axis=0
    )

    wide = (chans, 2 * chans)
    row_id = lax.broadcasted_iota(jnp.int32, (chans, chans), 0)
    col_id = lax.broadcasted_iota(jnp.int32, (chans, chans), 1)
    work = jnp.concatenate([gram, jnp.where(row_id == col_id, 1.0, 0.0)], axis=1)
    row_wide = lax.broadcasted_iota(jnp.int32, wide, 0)
    pivots = jnp.ones(wide, F32)
    panel = 4
    for k in range(0, chans, panel):
        rows = [jnp.broadcast_to(work[k + i : k + i + 1], wide) for i in range(panel)]
        columns = [
            jnp.broadcast_to(work[:, k + i : k + i + 1], wide) for i in range(panel)
        ]
        corner = [
            [jnp.broadcast_to(columns[j][k + i : k + i + 1], wide) for j in range(i + 1)]
            for i in range(panel)
        ]
        for j in range(panel):
            pivots = jnp.where(row_wide == k + j, corner[j][j], pivots)
            inverse_pivot = 1.0 / corner[j][j]
            factors = [corner[i][j] * inverse_pivot for i in range(j + 1, panel)]
            for i in range(j + 1, panel):
                factor = factors[i - j - 1]
                rows[i] = rows[i] - factor * rows[j]
                columns[i] = columns[i] - factor * columns[j]
                for m in range(j + 1, i + 1):
                    corner[i][m] = corner[i][m] - factor * corner[m][j]
            below = jnp.where(row_wide > k + j, columns[j], 0.0)
            work = work - below * (rows[j] * inverse_pivot)
    inverse = (work * lax.rsqrt(pivots))[:, chans:]
    ih, im, il = split3(inverse)
    lhs = jnp.concatenate([ih, im, il, ih, im, ih], axis=1)
    eh = emb_parts[:chans]
    em = emb_parts[chans : 2 * chans]
    el = emb_parts[2 * chans :]
    rhs = jnp.concatenate([eh, eh, eh, em, em, el], axis=0)
    out_ref[...] = jnp.dot(lhs, rhs, preferred_element_type=F32)

    probe_right.wait_send()
    probe_left.wait_send()
    raw_right.wait_send()
    raw_left.wait_send()
    for copy in part_copies:
        copy.wait_send()

    def drain(step, carry):
        wait_all(near_sums.at[step], near_send.at[step], group)
        wait_all(far_sums.at[step], far_send.at[step], groups)
        for side, at in ((0, 0), (1, 2 * blocks)):
            view = window.at[step, pl.ds(at, blocks)]
            pltpu.make_async_copy(view, view, win_send.at[step, side]).wait()
        return carry

    lax.fori_loop(0, POWER, drain, 0)
    wait_all(near_grams, gram_send.at[0], group)
    wait_all(far_grams, gram_send.at[1], groups)


def per_device(row_axis, col_axis, tile_blocks, tile_cols, tile_count, start_mass, probe_block):
    blocks, slots, tile = tile_blocks.shape[:3]
    chans = probe_block.shape[0]
    devices = row_axis * col_axis
    zones = blocks * tile
    halves = tile // 128
    vmem = pl.BlockSpec(memory_space=pltpu.VMEM)
    in_hbm = pl.BlockSpec(memory_space=pltpu.HBM)
    group = min(8, devices)
    groups = devices // group
    dma = pltpu.SemaphoreType.DMA
    part = pltpu.VMEM((halves, chans * blocks, 128), F32)
    return pl.pallas_call(
        functools.partial(kernel, row_axis, col_axis, group, blocks, slots, tile, chans),
        out_shape=jax.ShapeDtypeStruct((chans, zones), F32),
        in_specs=[in_hbm] * 5,
        out_specs=vmem,
        scratch_shapes=[
            pltpu.SMEM(tile_cols.shape, jnp.int32),
            pltpu.SMEM(tile_count.shape, jnp.int32),
            pltpu.VMEM(start_mass.shape, F32),
            pltpu.VMEM(probe_block.shape, BF16),
            pltpu.VMEM((blocks, slots, tile, tile), BF16),
            pltpu.VMEM((blocks, 4 * blocks, slots * tile), BF16),
            pltpu.VMEM((POWER, 3 * blocks, tile), F32),
            pltpu.VMEM((POWER, 2, blocks, tile), F32),
            pltpu.VMEM((3, blocks, tile), F32),
            pltpu.VMEM((POWER, group, 1, 128), F32),
            pltpu.VMEM((POWER, groups, 1, 128), F32),
            pltpu.VMEM((2, chans, zones), BF16),
            pltpu.VMEM((3 * blocks + 1, chans, tile), BF16),
            pltpu.VMEM((halves, blocks * slots * chans, 128), F32),
            part, part, part, part, part,
            pltpu.VMEM((3 * chans, zones), BF16),
            pltpu.VMEM((chans, zones), F32),
            pltpu.VMEM((group, 8, 128), F32),
            pltpu.VMEM((groups, 8, 128), F32),
            dma((4,)),
            dma((blocks,)),
            dma((POWER,)), dma((POWER,)),
            dma((POWER,)), dma((POWER,)),
            dma((POWER, 2)), dma((POWER, 2)),
            dma((2,)), dma((2,)),
            dma((2,)), dma((2,)),
            dma((2, halves)), dma((2, halves)),
            dma((2,)), dma((2,)),
        ],
        compiler_params=pltpu.CompilerParams(
            collective_id=0, has_side_effects=True, vmem_limit_bytes=64 * 1024 * 1024
        ),
        name="embed",
    )(tile_cols, tile_count, tile_blocks, start_mass, probe_block)


def solution(mesh):
    sizes = dict(mesh.shape)
    return jax.shard_map(
        functools.partial(per_device, sizes["rows"], sizes["cols"]),
        mesh=mesh,
        in_specs=(
            P(("rows", "cols"), None, None, None),
            P(("rows", "cols"), None),
            P(("rows", "cols")),
            P(("rows", "cols")),
            P(None, ("rows", "cols")),
        ),
        out_specs=P(None, ("rows", "cols")),
        check_vma=False,
    )
```

```python
import functools
import math

import jax
import jax.numpy as jnp
from jax import lax
from jax.experimental import pallas as pl
from jax.experimental.pallas import tpu as pltpu
from jax.sharding import PartitionSpec as P

POWER = 4
MESH = pl.DeviceIdType.MESH
F32 = jnp.float32
BF16 = jnp.bfloat16


def split3(value):
    high = value.astype(BF16)
    rest = value - high.astype(F32)
    middle = rest.astype(BF16)
    low = (rest - middle.astype(F32)).astype(BF16)
    return high, middle, low


def kernel(
    row_axis, col_axis, group, blocks, slots, tile, chans,
    cols_hbm, count_hbm, tiles_hbm, mass_hbm, probe_hbm, out_ref,
    cols_ref, count_ref, mass_ref, probe_ref,
    tiles, place, window, landed, raw_halo, sums, probe_halo, scaled, products,
    low, mid, up, from_left, from_right, emb_parts, embedded, near_grams, far_grams,
    small_sem, load_sem, sum_send, sum_recv,
    win_send, win_recv, halo_send, halo_recv,
    probe_send, probe_recv, part_send, part_recv, gram_send, gram_recv,
):
    devices = row_axis * col_axis
    me = lax.axis_index("rows") * col_axis + lax.axis_index("cols")
    right = lax.rem(me + 1, devices)
    left = lax.rem(me + devices - 1, devices)
    total_blocks = devices * blocks
    pairs = blocks * slots
    span = 4 * blocks
    groups = devices // group
    my_group = me // group
    my_member = lax.rem(me, group)

    def place_of(device):
        return (device // col_axis, lax.rem(device, col_axis))

    def remote(src, dst, send, recv, device):
        return pltpu.make_async_remote_copy(
            src_ref=src, dst_ref=dst, send_sem=send, recv_sem=recv,
            device_id=place_of(device), device_id_type=MESH,
        )

    smalls = [
        pltpu.make_async_copy(src, dst, small_sem.at[i])
        for i, (src, dst) in enumerate(
            ((cols_hbm, cols_ref), (count_hbm, count_ref), (probe_hbm, probe_ref), (mass_hbm, mass_ref))
        )
    ]
    for small in smalls:
        small.start()
    loads = [
        pltpu.make_async_copy(tiles_hbm.at[b], tiles.at[b], load_sem.at[b]) for b in range(blocks)
    ]
    for load in loads:
        load.start()

    barrier = pltpu.get_barrier_semaphore()

    def near(offset):
        return my_group * group + lax.rem(my_member + offset, group)

    def far(offset):
        return lax.rem(my_group + offset, groups) * group + my_member

    def greet(other):
        pl.semaphore_signal(barrier, inc=1, device_id=place_of(other), device_id_type=MESH)

    def each(count, action):
        def body(offset, carry):
            action(offset)
            return carry

        lax.fori_loop(1, count, body, 0, unroll=count <= 32)

    each(devices, lambda offset: greet(lax.rem(me + offset, devices)))
    smalls[0].wait()
    smalls[1].wait()

    first = me * blocks
    spot = []
    alive = []
    for b in range(blocks):
        for k in range(slots):
            at = cols_ref[b, k] - first + blocks
            at = jnp.where(at < 0, at + total_blocks, at)
            at = jnp.where(at >= total_blocks, at - total_blocks, at)
            live = k < count_ref[b]
            spot.append(jnp.where(live, at, 3 * blocks))
            alive.append(live)
    rows_iota = lax.broadcasted_iota(jnp.int32, (span, 128), 0)
    lane3 = lax.rem(lax.broadcasted_iota(jnp.int32, (8, 3 * pairs), 1), pairs)
    spot_row = jnp.zeros((8, 3 * pairs), jnp.int32)
    for s in range(pairs):
        hit = jnp.where(rows_iota == spot[s], 1.0, 0.0)
        hit = jnp.where(rows_iota < 3 * blocks, hit, 0.0).astype(BF16)
        k = s % slots
        for part in range(tile // 128):
            place[s // slots, :, k * tile + part * 128 : k * tile + (part + 1) * 128] = hit
        spot_row = jnp.where(lane3 == s, spot[s], spot_row)
    rows3 = lax.broadcasted_iota(jnp.int32, (span, 3 * pairs), 0)
    place3 = jnp.where(rows3 == spot_row[0:1], 1.0, 0.0).astype(BF16)
    scaled[3 * blocks] = jnp.zeros((chans, tile), BF16)

    smalls[2].wait()
    pl.semaphore_wait(barrier, devices - 1)

    probe_right = remote(probe_ref, probe_halo.at[0], probe_send.at[0], probe_recv.at[0], right)
    probe_left = remote(probe_ref, probe_halo.at[1], probe_send.at[1], probe_recv.at[1], left)
    probe_right.start()
    probe_left.start()

    contract_last = (((1,), (1,)), ((), ()))
    sum_rows = lax.broadcasted_iota(jnp.int32, (16, tile), 0)
    row_sum = jnp.zeros((16, tile), F32)
    for b in range(blocks):
        loads[b].wait()
        for k in range(slots):
            weight = jnp.where(alive[b * slots + k], 1.0, 0.0)
            chosen = jnp.where(sum_rows == b, weight, 0.0).astype(BF16)
            row_sum += lax.dot_general(
                chosen, tiles[b, k], contract_last, preferred_element_type=F32
            )
    row_inverse = 1.0 / row_sum[:blocks]

    def push_near(buffer, send, recv):
        each(
            group,
            lambda offset: remote(
                buffer.at[my_member], buffer.at[my_member], send, recv, near(offset)
            ).start(),
        )

    def push_far(buffer, send, recv):
        each(
            groups,
            lambda offset: remote(
                buffer.at[my_group], buffer.at[my_group], send, recv, far(offset)
            ).start(),
        )

    def wait_all(buffer, sem, count):
        view = buffer.at[pl.ds(0, count - 1)]
        pltpu.make_async_copy(view, view, sem).wait()

    def other(offset):
        return lax.rem(me + offset, devices)

    def norm_begin(step, raw):
        square = raw * raw
        folded = square[:, :128]
        for part in range(1, tile // 128):
            folded += square[:, part * 128 : (part + 1) * 128]
        sums[step, me] = jnp.sum(folded, axis=0, keepdims=True)
        each(
            devices,
            lambda offset: remote(
                sums.at[step, me], sums.at[step, me], sum_send.at[step], sum_recv.at[step],
                other(offset),
            ).start(),
        )

    def norm_end(step):
        wait_all(sums.at[step], sum_recv.at[step], devices)
        total = jnp.sum(jnp.sum(sums[step], axis=0), axis=1, keepdims=True)
        return math.sqrt(total_blocks * tile) / jnp.sqrt(total)

    def spread(step, mass):
        weighted = (mass * row_inverse).astype(BF16).astype(F32)
        total = jnp.zeros((span, tile), F32)
        for b in range(blocks):
            row = jnp.broadcast_to(weighted[b : b + 1], (span, tile)).astype(BF16)
            lhs = place[b] * jnp.concatenate([row] * slots, axis=1)
            total += jnp.dot(
                lhs, tiles[b].reshape(slots * tile, tile), preferred_element_type=F32
            )
        window[step] = total[: 3 * blocks]
        to_left = remote(
            window.at[step, pl.ds(0, blocks)], landed.at[step, 1],
            win_send.at[step, 0], win_recv.at[step, 1], left,
        )
        to_right = remote(
            window.at[step, pl.ds(2 * blocks, blocks)], landed.at[step, 0],
            win_send.at[step, 1], win_recv.at[step, 0], right,
        )
        to_left.start()
        to_right.start()
        to_left.wait_recv()
        to_right.wait_recv()
        arrived = total[blocks : 2 * blocks] + landed[step, 0] + landed[step, 1]
        return 0.85 * arrived + 0.15

    smalls[3].wait()
    start = jnp.concatenate(
        [mass_ref[pl.ds(b * tile, tile)].reshape(1, tile) for b in range(blocks)], axis=0
    )

    def power(step, mass):
        raw = spread(step, mass)
        norm_begin(step, raw)
        return raw * norm_end(step)

    raw = spread(POWER - 1, lax.fori_loop(0, POWER - 1, power, start))
    norm_begin(POWER - 1, raw)
    raw_halo[1] = raw
    raw_right = remote(raw_halo.at[1], raw_halo.at[0], halo_send.at[0], halo_recv.at[0], right)
    raw_left = remote(raw_halo.at[1], raw_halo.at[2], halo_send.at[1], halo_recv.at[1], left)
    raw_right.start()
    raw_left.start()
    norm = norm_end(POWER - 1)
    root = jnp.sqrt(raw * norm)
    root_inverse = 1.0 / root
    gain = root * row_inverse

    halves = tile // 128
    for b in range(blocks):
        probe = probe_ref[:, b * tile : (b + 1) * tile].astype(F32)
        pushed = (probe * gain[b : b + 1]).astype(BF16)
        for k in range(slots):
            product = jnp.dot(pushed, tiles[b, k], preferred_element_type=F32)
            at = (b * slots + k) * chans
            for h in range(halves):
                products[h, at : at + chans, :] = product[:, h * 128 : (h + 1) * 128]
    part_copies = []
    for chunk in range(2):
        begin, end = chunk * chans // 2, (chunk + 1) * chans // 2
        for c in range(begin, end):
            slab = jnp.concatenate(
                [products.at[h][pl.ds(c, pairs, stride=chans), :] for h in range(halves)], axis=1
            )
            parts = jnp.concatenate(split3(slab), axis=0)
            placed = jnp.dot(place3, parts, preferred_element_type=F32)
            for h in range(halves):
                column = placed[:, h * 128 : (h + 1) * 128]
                low[h, c * blocks : (c + 1) * blocks, :] = column[:blocks]
                mid[h, c * blocks : (c + 1) * blocks, :] = column[blocks : 2 * blocks]
                up[h, c * blocks : (c + 1) * blocks, :] = column[2 * blocks : 3 * blocks]
        some = pl.ds(begin * blocks, (end - begin) * blocks)
        to_left = remote(
            low.at[:, some], from_right.at[:, some],
            part_send.at[0, chunk], part_recv.at[0, chunk], left,
        )
        to_right = remote(
            up.at[:, some], from_left.at[:, some],
            part_send.at[1, chunk], part_recv.at[1, chunk], right,
        )
        to_left.start()
        to_right.start()
        part_copies += [to_left, to_right]

    probe_right.wait_recv()
    probe_left.wait_recv()
    raw_right.wait_recv()
    raw_left.wait_recv()
    for side, part in ((0, 0), (1, None), (2, 1)):
        if part is None:
            inverse = root_inverse
        else:
            inverse = 1.0 / jnp.sqrt(raw_halo[side] * norm)
        for b in range(blocks):
            lanes = slice(b * tile, (b + 1) * tile)
            probe = probe_ref[:, lanes] if part is None else probe_halo[part, :, lanes]
            scaled[side * blocks + b] = (probe.astype(F32) * inverse[b : b + 1]).astype(BF16)
    for b in range(blocks):
        forward = jnp.zeros((chans, tile), F32)
        for k in range(slots):
            forward += lax.dot_general(
                scaled[spot[b * slots + k]], tiles[b, k], contract_last,
                preferred_element_type=F32,
            )
        embedded[:, b * tile : (b + 1) * tile] = forward * gain[b : b + 1]

    for copy in part_copies:
        copy.wait_recv()
    for b in range(blocks):
        for h in range(halves):
            lanes = slice(b * tile + h * 128, b * tile + (h + 1) * 128)
            rows = pl.ds(b, chans, stride=blocks)
            arrived = mid.at[h][rows, :] + from_left.at[h][rows, :] + from_right.at[h][rows, :]
            back = arrived * root_inverse[b : b + 1, h * 128 : (h + 1) * 128]
            value = 0.5 * (embedded[:, lanes] + back)
            for index, piece in enumerate(split3(value)):
                emb_parts[index * chans : (index + 1) * chans, lanes] = piece

    cross = lax.dot_general(
        emb_parts[...], emb_parts[...], contract_last, preferred_element_type=F32
    )
    gram = jnp.zeros((chans, chans), F32)
    for i, j in ((2, 2), (1, 2), (2, 1), (0, 2), (2, 0), (1, 1), (0, 1), (1, 0), (0, 0)):
        gram += cross[i * chans : (i + 1) * chans, j * chans : (j + 1) * chans]
    quarters = chans // 8
    near_grams[my_member] = jnp.concatenate(
        [gram[q * 8 : (q + 1) * 8] for q in range(quarters)], axis=1
    )
    push_near(near_grams, gram_send.at[0], gram_recv.at[0])
    wait_all(near_grams, gram_recv.at[0], group)
    far_grams[my_group] = jnp.sum(near_grams[...], axis=0)
    push_far(far_grams, gram_send.at[1], gram_recv.at[1])
    wait_all(far_grams, gram_recv.at[1], groups)
    packed = jnp.sum(far_grams[...], axis=0)
    gram = jnp.concatenate(
        [packed[:, q * chans : (q + 1) * chans] for q in range(quarters)], axis=0
    )

    wide = (chans, 2 * chans)
    row_id = lax.broadcasted_iota(jnp.int32, (chans, chans), 0)
    col_id = lax.broadcasted_iota(jnp.int32, (chans, chans), 1)
    work = jnp.concatenate([gram, jnp.where(row_id == col_id, 1.0, 0.0)], axis=1)
    row_wide = lax.broadcasted_iota(jnp.int32, wide, 0)
    pivots = jnp.ones(wide, F32)
    panel = 4
    for k in range(0, chans, panel):
        rows = [jnp.broadcast_to(work[k + i : k + i + 1], wide) for i in range(panel)]
        columns = [
            jnp.broadcast_to(work[:, k + i : k + i + 1], wide) for i in range(panel)
        ]
        corner = [
            [jnp.broadcast_to(columns[j][k + i : k + i + 1], wide) for j in range(i + 1)]
            for i in range(panel)
        ]
        for j in range(panel):
            pivots = jnp.where(row_wide == k + j, corner[j][j], pivots)
            inverse_pivot = 1.0 / corner[j][j]
            factors = [corner[i][j] * inverse_pivot for i in range(j + 1, panel)]
            for i in range(j + 1, panel):
                factor = factors[i - j - 1]
                rows[i] = rows[i] - factor * rows[j]
                columns[i] = columns[i] - factor * columns[j]
                for m in range(j + 1, i + 1):
                    corner[i][m] = corner[i][m] - factor * corner[m][j]
            below = jnp.where(row_wide > k + j, columns[j], 0.0)
            work = work - below * (rows[j] * inverse_pivot)
    inverse = (work * lax.rsqrt(pivots))[:, chans:]
    ih, im, il = split3(inverse)
    lhs = jnp.concatenate([ih, im, il, ih, im, ih], axis=1)
    eh = emb_parts[:chans]
    em = emb_parts[chans : 2 * chans]
    el = emb_parts[2 * chans :]
    rhs = jnp.concatenate([eh, eh, eh, em, em, el], axis=0)
    out_ref[...] = jnp.dot(lhs, rhs, preferred_element_type=F32)

    probe_right.wait_send()
    probe_left.wait_send()
    raw_right.wait_send()
    raw_left.wait_send()
    for copy in part_copies:
        copy.wait_send()

    def drain(step, carry):
        wait_all(sums.at[step], sum_send.at[step], devices)
        for side, at in ((0, 0), (1, 2 * blocks)):
            view = window.at[step, pl.ds(at, blocks)]
            pltpu.make_async_copy(view, view, win_send.at[step, side]).wait()
        return carry

    lax.fori_loop(0, POWER, drain, 0)
    wait_all(near_grams, gram_send.at[0], group)
    wait_all(far_grams, gram_send.at[1], groups)


def per_device(row_axis, col_axis, tile_blocks, tile_cols, tile_count, start_mass, probe_block):
    blocks, slots, tile = tile_blocks.shape[:3]
    chans = probe_block.shape[0]
    devices = row_axis * col_axis
    zones = blocks * tile
    halves = tile // 128
    vmem = pl.BlockSpec(memory_space=pltpu.VMEM)
    in_hbm = pl.BlockSpec(memory_space=pltpu.HBM)
    group = min(8, devices)
    groups = devices // group
    dma = pltpu.SemaphoreType.DMA
    part = pltpu.VMEM((halves, chans * blocks, 128), F32)
    return pl.pallas_call(
        functools.partial(kernel, row_axis, col_axis, group, blocks, slots, tile, chans),
        out_shape=jax.ShapeDtypeStruct((chans, zones), F32),
        in_specs=[in_hbm] * 5,
        out_specs=vmem,
        scratch_shapes=[
            pltpu.SMEM(tile_cols.shape, jnp.int32),
            pltpu.SMEM(tile_count.shape, jnp.int32),
            pltpu.VMEM(start_mass.shape, F32),
            pltpu.VMEM(probe_block.shape, BF16),
            pltpu.VMEM((blocks, slots, tile, tile), BF16),
            pltpu.VMEM((blocks, 4 * blocks, slots * tile), BF16),
            pltpu.VMEM((POWER, 3 * blocks, tile), F32),
            pltpu.VMEM((POWER, 2, blocks, tile), F32),
            pltpu.VMEM((3, blocks, tile), F32),
            pltpu.VMEM((POWER, devices, 1, 128), F32),
            pltpu.VMEM((2, chans, zones), BF16),
            pltpu.VMEM((3 * blocks + 1, chans, tile), BF16),
            pltpu.VMEM((halves, blocks * slots * chans, 128), F32),
            part, part, part, part, part,
            pltpu.VMEM((3 * chans, zones), BF16),
            pltpu.VMEM((chans, zones), F32),
            pltpu.VMEM((group, 8, 128), F32),
            pltpu.VMEM((groups, 8, 128), F32),
            dma((4,)),
            dma((blocks,)),
            dma((POWER,)), dma((POWER,)),
            dma((POWER, 2)), dma((POWER, 2)),
            dma((2,)), dma((2,)),
            dma((2,)), dma((2,)),
            dma((2, 2)), dma((2, 2)),
            dma((2,)), dma((2,)),
        ],
        compiler_params=pltpu.CompilerParams(
            collective_id=0, has_side_effects=True, vmem_limit_bytes=64 * 1024 * 1024
        ),
        name="embed",
    )(tile_cols, tile_count, tile_blocks, start_mass, probe_block)


def solution(mesh):
    sizes = dict(mesh.shape)
    return jax.shard_map(
        functools.partial(per_device, sizes["rows"], sizes["cols"]),
        mesh=mesh,
        in_specs=(
            P(("rows", "cols"), None, None, None),
            P(("rows", "cols"), None),
            P(("rows", "cols")),
            P(("rows", "cols")),
            P(None, ("rows", "cols")),
        ),
        out_specs=P(None, ("rows", "cols")),
        check_vma=False,
    )
```

```python
import functools
import math

import jax
import jax.numpy as jnp
from jax import lax
from jax.experimental import pallas as pl
from jax.experimental.pallas import tpu as pltpu
from jax.sharding import PartitionSpec as P

POWER = 4
MESH = pl.DeviceIdType.MESH
F32 = jnp.float32
BF16 = jnp.bfloat16


def split3(value):
    high = value.astype(BF16)
    rest = value - high.astype(F32)
    middle = rest.astype(BF16)
    low = (rest - middle.astype(F32)).astype(BF16)
    return high, middle, low


def kernel(
    row_axis, col_axis, group, blocks, slots, tile, chans,
    cols_hbm, count_hbm, tiles_hbm, mass_hbm, probe_hbm, out_ref,
    cols_ref, count_ref, mass_ref, probe_ref,
    tiles, place, window, landed, raw_halo, sums, probe_halo, scaled, products,
    low, mid, up, from_left, from_right, emb_parts, embedded, near_grams, far_grams,
    small_sem, load_sem, sum_send, sum_recv,
    win_send, win_recv, halo_send, halo_recv,
    probe_send, probe_recv, part_send, part_recv, gram_send, gram_recv,
):
    devices = row_axis * col_axis
    me = lax.axis_index("rows") * col_axis + lax.axis_index("cols")
    right = lax.rem(me + 1, devices)
    left = lax.rem(me + devices - 1, devices)
    total_blocks = devices * blocks
    pairs = blocks * slots
    span = 4 * blocks
    groups = devices // group
    my_group = me // group
    my_member = lax.rem(me, group)

    def place_of(device):
        return (device // col_axis, lax.rem(device, col_axis))

    def remote(src, dst, send, recv, device):
        return pltpu.make_async_remote_copy(
            src_ref=src, dst_ref=dst, send_sem=send, recv_sem=recv,
            device_id=place_of(device), device_id_type=MESH,
        )

    smalls = [
        pltpu.make_async_copy(src, dst, small_sem.at[i])
        for i, (src, dst) in enumerate(
            ((cols_hbm, cols_ref), (count_hbm, count_ref), (probe_hbm, probe_ref), (mass_hbm, mass_ref))
        )
    ]
    for small in smalls:
        small.start()
    loads = [
        pltpu.make_async_copy(tiles_hbm.at[b], tiles.at[b], load_sem.at[b]) for b in range(blocks)
    ]
    for load in loads:
        load.start()

    barrier = pltpu.get_barrier_semaphore()

    def near(offset):
        return my_group * group + lax.rem(my_member + offset, group)

    def far(offset):
        return lax.rem(my_group + offset, groups) * group + my_member

    def greet(other):
        pl.semaphore_signal(barrier, inc=1, device_id=place_of(other), device_id_type=MESH)

    def each(count, action):
        def body(offset, carry):
            action(offset)
            return carry

        lax.fori_loop(1, count, body, 0, unroll=count <= 32)

    each(devices, lambda offset: greet(lax.rem(me + offset, devices)))
    smalls[0].wait()
    smalls[1].wait()

    first = me * blocks
    spot = []
    alive = []
    for b in range(blocks):
        for k in range(slots):
            at = cols_ref[b, k] - first + blocks
            at = jnp.where(at < 0, at + total_blocks, at)
            at = jnp.where(at >= total_blocks, at - total_blocks, at)
            live = k < count_ref[b]
            spot.append(jnp.where(live, at, 3 * blocks))
            alive.append(live)
    rows_iota = lax.broadcasted_iota(jnp.int32, (span, 128), 0)
    lane3 = lax.rem(lax.broadcasted_iota(jnp.int32, (8, 3 * pairs), 1), pairs)
    spot_row = jnp.zeros((8, 3 * pairs), jnp.int32)
    for s in range(pairs):
        hit = jnp.where(rows_iota == spot[s], 1.0, 0.0)
        hit = jnp.where(rows_iota < 3 * blocks, hit, 0.0).astype(BF16)
        k = s % slots
        for part in range(tile // 128):
            place[s // slots, :, k * tile + part * 128 : k * tile + (part + 1) * 128] = hit
        spot_row = jnp.where(lane3 == s, spot[s], spot_row)
    rows3 = lax.broadcasted_iota(jnp.int32, (span, 3 * pairs), 0)
    place3 = jnp.where(rows3 == spot_row[0:1], 1.0, 0.0).astype(BF16)
    scaled[3 * blocks * chans // 128] = jnp.zeros((tile, 128), BF16)

    smalls[2].wait()
    pl.semaphore_wait(barrier, devices - 1)

    probe_right = remote(probe_ref, probe_halo.at[0], probe_send.at[0], probe_recv.at[0], right)
    probe_left = remote(probe_ref, probe_halo.at[1], probe_send.at[1], probe_recv.at[1], left)
    probe_right.start()
    probe_left.start()

    contract_last = (((1,), (1,)), ((), ()))
    lane = lax.broadcasted_iota(jnp.int32, (tile, 128), 1)
    ones = jnp.ones((tile, 128), BF16)
    columns = jnp.zeros((tile, 128), F32)
    for b in range(blocks):
        loads[b].wait()
        own = jnp.zeros((tile, 128), F32)
        for k in range(slots):
            weight = jnp.where(alive[b * slots + k], 1.0, 0.0)
            own += weight * jnp.dot(tiles[b, k], ones, preferred_element_type=F32)
        columns = jnp.where(lane == b, own, columns)
    row_sum = columns.T
    row_inverse = 1.0 / row_sum[:blocks]

    def push_near(buffer, send, recv):
        each(
            group,
            lambda offset: remote(
                buffer.at[my_member], buffer.at[my_member], send, recv, near(offset)
            ).start(),
        )

    def push_far(buffer, send, recv):
        each(
            groups,
            lambda offset: remote(
                buffer.at[my_group], buffer.at[my_group], send, recv, far(offset)
            ).start(),
        )

    def wait_all(buffer, sem, count):
        view = buffer.at[pl.ds(0, count - 1)]
        pltpu.make_async_copy(view, view, sem).wait()

    def other(offset):
        return lax.rem(me + offset, devices)

    def norm_begin(step, raw):
        square = raw * raw
        folded = square[:, :128]
        for part in range(1, tile // 128):
            folded += square[:, part * 128 : (part + 1) * 128]
        sums[step, me] = jnp.sum(folded, axis=0, keepdims=True)
        each(
            devices,
            lambda offset: remote(
                sums.at[step, me], sums.at[step, me], sum_send.at[step], sum_recv.at[step],
                other(offset),
            ).start(),
        )

    def norm_end(step):
        wait_all(sums.at[step], sum_recv.at[step], devices)
        total = jnp.sum(jnp.sum(sums[step], axis=0), axis=1, keepdims=True)
        return math.sqrt(total_blocks * tile) / jnp.sqrt(total)

    def spread(step, mass):
        weighted = (mass * row_inverse).astype(BF16).astype(F32)
        total = jnp.zeros((span, tile), F32)
        for b in range(blocks):
            row = jnp.broadcast_to(weighted[b : b + 1], (span, tile)).astype(BF16)
            lhs = place[b] * jnp.concatenate([row] * slots, axis=1)
            total += jnp.dot(
                lhs, tiles[b].reshape(slots * tile, tile), preferred_element_type=F32
            )
        window[step] = total[: 3 * blocks]
        to_left = remote(
            window.at[step, pl.ds(0, blocks)], landed.at[step, 1],
            win_send.at[step, 0], win_recv.at[step, 1], left,
        )
        to_right = remote(
            window.at[step, pl.ds(2 * blocks, blocks)], landed.at[step, 0],
            win_send.at[step, 1], win_recv.at[step, 0], right,
        )
        to_left.start()
        to_right.start()
        to_left.wait_recv()
        to_right.wait_recv()
        arrived = total[blocks : 2 * blocks] + landed[step, 0] + landed[step, 1]
        return 0.85 * arrived + 0.15

    smalls[3].wait()
    start = jnp.concatenate(
        [mass_ref[pl.ds(b * tile, tile)].reshape(1, tile) for b in range(blocks)], axis=0
    )

    def power(step, mass):
        raw = spread(step, mass)
        norm_begin(step, raw)
        return raw * norm_end(step)

    raw = spread(POWER - 1, lax.fori_loop(0, POWER - 1, power, start))
    norm_begin(POWER - 1, raw)
    raw_halo[1] = raw
    raw_right = remote(raw_halo.at[1], raw_halo.at[0], halo_send.at[0], halo_recv.at[0], right)
    raw_left = remote(raw_halo.at[1], raw_halo.at[2], halo_send.at[1], halo_recv.at[1], left)
    raw_right.start()
    raw_left.start()
    norm = norm_end(POWER - 1)
    root = jnp.sqrt(raw * norm)
    root_inverse = 1.0 / root
    gain = root * row_inverse

    halves = tile // 128
    for b in range(blocks):
        probe = probe_ref[:, b * tile : (b + 1) * tile].astype(F32)
        pushed = (probe * gain[b : b + 1]).astype(BF16)
        for k in range(slots):
            product = jnp.dot(pushed, tiles[b, k], preferred_element_type=F32)
            at = (b * slots + k) * chans
            for h in range(halves):
                products[h, at : at + chans, :] = product[:, h * 128 : (h + 1) * 128]
    part_copies = []
    for chunk in range(2):
        begin, end = chunk * chans // 2, (chunk + 1) * chans // 2
        for c in range(begin, end):
            slab = jnp.concatenate(
                [products.at[h][pl.ds(c, pairs, stride=chans), :] for h in range(halves)], axis=1
            )
            parts = jnp.concatenate(split3(slab), axis=0)
            placed = jnp.dot(place3, parts, preferred_element_type=F32)
            for h in range(halves):
                column = placed[:, h * 128 : (h + 1) * 128]
                low[h, c * blocks : (c + 1) * blocks, :] = column[:blocks]
                mid[h, c * blocks : (c + 1) * blocks, :] = column[blocks : 2 * blocks]
                up[h, c * blocks : (c + 1) * blocks, :] = column[2 * blocks : 3 * blocks]
        some = pl.ds(begin * blocks, (end - begin) * blocks)
        to_left = remote(
            low.at[:, some], from_right.at[:, some],
            part_send.at[0, chunk], part_recv.at[0, chunk], left,
        )
        to_right = remote(
            up.at[:, some], from_left.at[:, some],
            part_send.at[1, chunk], part_recv.at[1, chunk], right,
        )
        to_left.start()
        to_right.start()
        part_copies += [to_left, to_right]

    probe_right.wait_recv()
    probe_left.wait_recv()
    raw_right.wait_recv()
    raw_left.wait_recv()
    quads = 128 // chans
    pieces = []
    for side, part in ((0, 0), (1, None), (2, 1)):
        if part is None:
            inverse = root_inverse
        else:
            inverse = 1.0 / jnp.sqrt(raw_halo[side] * norm)
        for b in range(blocks):
            lanes = slice(b * tile, (b + 1) * tile)
            probe = probe_ref[:, lanes] if part is None else probe_halo[part, :, lanes]
            pieces.append(probe.astype(F32) * inverse[b : b + 1])
            if len(pieces) == quads:
                at = (side * blocks + b) // quads
                scaled[at] = jnp.concatenate(pieces, axis=0).T.astype(BF16)
                pieces = []
    quad_lane = lax.broadcasted_iota(jnp.int32, (16, 128), 1) // chans
    for b in range(blocks):
        sums_up = jnp.zeros((tile, 128), F32)
        for k in range(slots):
            at = spot[b * slots + k]
            pick = jnp.where(quad_lane == lax.rem(at, quads), 1.0, 0.0).astype(BF16)
            chosen = scaled[at // quads] * jnp.concatenate([pick] * (tile // 16), axis=0)
            sums_up += jnp.dot(tiles[b, k], chosen, preferred_element_type=F32)
        turned = sums_up.T
        forward = turned[:chans]
        for q in range(1, quads):
            forward += turned[q * chans : (q + 1) * chans]
        embedded[:, b * tile : (b + 1) * tile] = forward * gain[b : b + 1]

    for copy in part_copies:
        copy.wait_recv()
    for b in range(blocks):
        for h in range(halves):
            lanes = slice(b * tile + h * 128, b * tile + (h + 1) * 128)
            rows = pl.ds(b, chans, stride=blocks)
            arrived = mid.at[h][rows, :] + from_left.at[h][rows, :] + from_right.at[h][rows, :]
            back = arrived * root_inverse[b : b + 1, h * 128 : (h + 1) * 128]
            value = 0.5 * (embedded[:, lanes] + back)
            for index, piece in enumerate(split3(value)):
                emb_parts[index * chans : (index + 1) * chans, lanes] = piece

    cross = lax.dot_general(
        emb_parts[...], emb_parts[...], contract_last, preferred_element_type=F32
    )
    gram = jnp.zeros((chans, chans), F32)
    for i, j in ((2, 2), (1, 2), (2, 1), (0, 2), (2, 0), (1, 1), (0, 1), (1, 0), (0, 0)):
        gram += cross[i * chans : (i + 1) * chans, j * chans : (j + 1) * chans]
    quarters = chans // 8
    near_grams[my_member] = jnp.concatenate(
        [gram[q * 8 : (q + 1) * 8] for q in range(quarters)], axis=1
    )
    push_near(near_grams, gram_send.at[0], gram_recv.at[0])
    wait_all(near_grams, gram_recv.at[0], group)
    far_grams[my_group] = jnp.sum(near_grams[...], axis=0)
    push_far(far_grams, gram_send.at[1], gram_recv.at[1])
    wait_all(far_grams, gram_recv.at[1], groups)
    packed = jnp.sum(far_grams[...], axis=0)
    gram = jnp.concatenate(
        [packed[:, q * chans : (q + 1) * chans] for q in range(quarters)], axis=0
    )

    wide = (chans, 2 * chans)
    row_id = lax.broadcasted_iota(jnp.int32, (chans, chans), 0)
    col_id = lax.broadcasted_iota(jnp.int32, (chans, chans), 1)
    work = jnp.concatenate([gram, jnp.where(row_id == col_id, 1.0, 0.0)], axis=1)
    row_wide = lax.broadcasted_iota(jnp.int32, wide, 0)
    pivots = jnp.ones(wide, F32)
    panel = 4
    for k in range(0, chans, panel):
        rows = [jnp.broadcast_to(work[k + i : k + i + 1], wide) for i in range(panel)]
        columns = [
            jnp.broadcast_to(work[:, k + i : k + i + 1], wide) for i in range(panel)
        ]
        corner = [
            [jnp.broadcast_to(columns[j][k + i : k + i + 1], wide) for j in range(i + 1)]
            for i in range(panel)
        ]
        for j in range(panel):
            pivots = jnp.where(row_wide == k + j, corner[j][j], pivots)
            inverse_pivot = 1.0 / corner[j][j]
            factors = [corner[i][j] * inverse_pivot for i in range(j + 1, panel)]
            for i in range(j + 1, panel):
                factor = factors[i - j - 1]
                rows[i] = rows[i] - factor * rows[j]
                columns[i] = columns[i] - factor * columns[j]
                for m in range(j + 1, i + 1):
                    corner[i][m] = corner[i][m] - factor * corner[m][j]
            below = jnp.where(row_wide > k + j, columns[j], 0.0)
            work = work - below * (rows[j] * inverse_pivot)
    inverse = (work * lax.rsqrt(pivots))[:, chans:]
    ih, im, il = split3(inverse)
    lhs = jnp.concatenate([ih, im, il, ih, im, ih], axis=1)
    eh = emb_parts[:chans]
    em = emb_parts[chans : 2 * chans]
    el = emb_parts[2 * chans :]
    rhs = jnp.concatenate([eh, eh, eh, em, em, el], axis=0)
    out_ref[...] = jnp.dot(lhs, rhs, preferred_element_type=F32)

    probe_right.wait_send()
    probe_left.wait_send()
    raw_right.wait_send()
    raw_left.wait_send()
    for copy in part_copies:
        copy.wait_send()

    def drain(step, carry):
        wait_all(sums.at[step], sum_send.at[step], devices)
        for side, at in ((0, 0), (1, 2 * blocks)):
            view = window.at[step, pl.ds(at, blocks)]
            pltpu.make_async_copy(view, view, win_send.at[step, side]).wait()
        return carry

    lax.fori_loop(0, POWER, drain, 0)
    wait_all(near_grams, gram_send.at[0], group)
    wait_all(far_grams, gram_send.at[1], groups)


def per_device(row_axis, col_axis, tile_blocks, tile_cols, tile_count, start_mass, probe_block):
    blocks, slots, tile = tile_blocks.shape[:3]
    chans = probe_block.shape[0]
    devices = row_axis * col_axis
    zones = blocks * tile
    halves = tile // 128
    vmem = pl.BlockSpec(memory_space=pltpu.VMEM)
    in_hbm = pl.BlockSpec(memory_space=pltpu.HBM)
    group = min(8, devices)
    groups = devices // group
    dma = pltpu.SemaphoreType.DMA
    part = pltpu.VMEM((halves, chans * blocks, 128), F32)
    return pl.pallas_call(
        functools.partial(kernel, row_axis, col_axis, group, blocks, slots, tile, chans),
        out_shape=jax.ShapeDtypeStruct((chans, zones), F32),
        in_specs=[in_hbm] * 5,
        out_specs=vmem,
        scratch_shapes=[
            pltpu.SMEM(tile_cols.shape, jnp.int32),
            pltpu.SMEM(tile_count.shape, jnp.int32),
            pltpu.VMEM(start_mass.shape, F32),
            pltpu.VMEM(probe_block.shape, BF16),
            pltpu.VMEM((blocks, slots, tile, tile), BF16),
            pltpu.VMEM((blocks, 4 * blocks, slots * tile), BF16),
            pltpu.VMEM((POWER, 3 * blocks, tile), F32),
            pltpu.VMEM((POWER, 2, blocks, tile), F32),
            pltpu.VMEM((3, blocks, tile), F32),
            pltpu.VMEM((POWER, devices, 1, 128), F32),
            pltpu.VMEM((2, chans, zones), BF16),
            pltpu.VMEM((3 * blocks * chans // 128 + 1, tile, 128), BF16),
            pltpu.VMEM((halves, blocks * slots * chans, 128), F32),
            part, part, part, part, part,
            pltpu.VMEM((3 * chans, zones), BF16),
            pltpu.VMEM((chans, zones), F32),
            pltpu.VMEM((group, 8, 128), F32),
            pltpu.VMEM((groups, 8, 128), F32),
            dma((4,)),
            dma((blocks,)),
            dma((POWER,)), dma((POWER,)),
            dma((POWER, 2)), dma((POWER, 2)),
            dma((2,)), dma((2,)),
            dma((2,)), dma((2,)),
            dma((2, 2)), dma((2, 2)),
            dma((2,)), dma((2,)),
        ],
        compiler_params=pltpu.CompilerParams(
            collective_id=0, has_side_effects=True, vmem_limit_bytes=64 * 1024 * 1024
        ),
        name="embed",
    )(tile_cols, tile_count, tile_blocks, start_mass, probe_block)


def solution(mesh):
    sizes = dict(mesh.shape)
    return jax.shard_map(
        functools.partial(per_device, sizes["rows"], sizes["cols"]),
        mesh=mesh,
        in_specs=(
            P(("rows", "cols"), None, None, None),
            P(("rows", "cols"), None),
            P(("rows", "cols")),
            P(("rows", "cols")),
            P(None, ("rows", "cols")),
        ),
        out_specs=P(None, ("rows", "cols")),
        check_vma=False,
    )
```

```python
import functools
import math

import jax
import jax.numpy as jnp
from jax import lax
from jax.experimental import pallas as pl
from jax.experimental.pallas import tpu as pltpu
from jax.sharding import PartitionSpec as P

POWER = 4
MESH = pl.DeviceIdType.MESH
F32 = jnp.float32
BF16 = jnp.bfloat16


def split3(value):
    high = value.astype(BF16)
    rest = value - high.astype(F32)
    middle = rest.astype(BF16)
    low = (rest - middle.astype(F32)).astype(BF16)
    return high, middle, low


def kernel(
    row_axis, col_axis, blocks, slots, tile, chans,
    cols_hbm, count_hbm, tiles_hbm, mass_hbm, probe_hbm, out_ref,
    cols_ref, count_ref, mass_ref, probe_ref,
    tiles, place, window, landed, raw_halo, sums, probe_halo, scaled, products,
    low, mid, up, from_left, from_right, emb_parts, embedded, grams,
    small_sem, load_sem, sum_send, sum_recv,
    win_send, win_recv, halo_send, halo_recv,
    probe_send, probe_recv, part_send, part_recv, gram_send, gram_recv,
):
    devices = row_axis * col_axis
    me = lax.axis_index("rows") * col_axis + lax.axis_index("cols")
    right = lax.rem(me + 1, devices)
    left = lax.rem(me + devices - 1, devices)
    total_blocks = devices * blocks
    pairs = blocks * slots
    span = 4 * blocks

    def place_of(device):
        return (device // col_axis, lax.rem(device, col_axis))

    def remote(src, dst, send, recv, device):
        return pltpu.make_async_remote_copy(
            src_ref=src, dst_ref=dst, send_sem=send, recv_sem=recv,
            device_id=place_of(device), device_id_type=MESH,
        )

    smalls = [
        pltpu.make_async_copy(src, dst, small_sem.at[i])
        for i, (src, dst) in enumerate(
            ((cols_hbm, cols_ref), (count_hbm, count_ref), (probe_hbm, probe_ref), (mass_hbm, mass_ref))
        )
    ]
    for small in smalls:
        small.start()
    loads = [
        pltpu.make_async_copy(tiles_hbm.at[b], tiles.at[b], load_sem.at[b]) for b in range(blocks)
    ]
    for load in loads:
        load.start()

    barrier = pltpu.get_barrier_semaphore()

    def greet(other):
        pl.semaphore_signal(barrier, inc=1, device_id=place_of(other), device_id_type=MESH)

    def each(count, action):
        def body(offset, carry):
            action(offset)
            return carry

        lax.fori_loop(1, count, body, 0, unroll=count <= 32)

    each(devices, lambda offset: greet(lax.rem(me + offset, devices)))
    smalls[0].wait()
    smalls[1].wait()

    first = me * blocks
    spot = []
    alive = []
    for b in range(blocks):
        for k in range(slots):
            at = cols_ref[b, k] - first + blocks
            at = jnp.where(at < 0, at + total_blocks, at)
            at = jnp.where(at >= total_blocks, at - total_blocks, at)
            live = k < count_ref[b]
            spot.append(jnp.where(live, at, 3 * blocks))
            alive.append(live)
    rows_iota = lax.broadcasted_iota(jnp.int32, (span, 128), 0)
    lane3 = lax.rem(lax.broadcasted_iota(jnp.int32, (8, 3 * pairs), 1), pairs)
    spot_row = jnp.zeros((8, 3 * pairs), jnp.int32)
    for s in range(pairs):
        hit = jnp.where(rows_iota == spot[s], 1.0, 0.0)
        hit = jnp.where(rows_iota < 3 * blocks, hit, 0.0).astype(BF16)
        k = s % slots
        for part in range(tile // 128):
            place[s // slots, :, k * tile + part * 128 : k * tile + (part + 1) * 128] = hit
        spot_row = jnp.where(lane3 == s, spot[s], spot_row)
    rows3 = lax.broadcasted_iota(jnp.int32, (span, 3 * pairs), 0)
    place3 = jnp.where(rows3 == spot_row[0:1], 1.0, 0.0).astype(BF16)
    scaled[3 * blocks * chans // 128] = jnp.zeros((tile, 128), BF16)

    smalls[2].wait()
    pl.semaphore_wait(barrier, devices - 1)

    probe_right = remote(probe_ref, probe_halo.at[0], probe_send.at[0], probe_recv.at[0], right)
    probe_left = remote(probe_ref, probe_halo.at[1], probe_send.at[1], probe_recv.at[1], left)
    probe_right.start()
    probe_left.start()

    contract_last = (((1,), (1,)), ((), ()))
    lane = lax.broadcasted_iota(jnp.int32, (tile, 128), 1)
    ones = jnp.ones((tile, 128), BF16)
    columns = jnp.zeros((tile, 128), F32)
    for b in range(blocks):
        loads[b].wait()
        own = jnp.zeros((tile, 128), F32)
        for k in range(slots):
            weight = jnp.where(alive[b * slots + k], 1.0, 0.0)
            own += weight * jnp.dot(tiles[b, k], ones, preferred_element_type=F32)
        columns = jnp.where(lane == b, own, columns)
    row_sum = columns.T
    row_inverse = 1.0 / row_sum[:blocks]

    def wait_all(buffer, sem, count):
        view = buffer.at[pl.ds(0, count - 1)]
        pltpu.make_async_copy(view, view, sem).wait()

    def other(offset):
        return lax.rem(me + offset, devices)

    def norm_begin(step, raw):
        square = raw * raw
        folded = square[:, :128]
        for part in range(1, tile // 128):
            folded += square[:, part * 128 : (part + 1) * 128]
        sums[step, me] = jnp.sum(folded, axis=0, keepdims=True)
        each(
            devices,
            lambda offset: remote(
                sums.at[step, me], sums.at[step, me], sum_send.at[step], sum_recv.at[step],
                other(offset),
            ).start(),
        )

    def norm_end(step):
        wait_all(sums.at[step], sum_recv.at[step], devices)
        total = jnp.sum(jnp.sum(sums[step], axis=0), axis=1, keepdims=True)
        return math.sqrt(total_blocks * tile) / jnp.sqrt(total)

    def spread(step, mass):
        weighted = (mass * row_inverse).astype(BF16).astype(F32)
        total = jnp.zeros((span, tile), F32)
        for b in range(blocks):
            row = jnp.broadcast_to(weighted[b : b + 1], (span, tile)).astype(BF16)
            lhs = place[b] * jnp.concatenate([row] * slots, axis=1)
            total += jnp.dot(
                lhs, tiles[b].reshape(slots * tile, tile), preferred_element_type=F32
            )
        window[step] = total[: 3 * blocks]
        to_left = remote(
            window.at[step, pl.ds(0, blocks)], landed.at[step, 1],
            win_send.at[step, 0], win_recv.at[step, 1], left,
        )
        to_right = remote(
            window.at[step, pl.ds(2 * blocks, blocks)], landed.at[step, 0],
            win_send.at[step, 1], win_recv.at[step, 0], right,
        )
        to_left.start()
        to_right.start()
        to_left.wait_recv()
        to_right.wait_recv()
        arrived = total[blocks : 2 * blocks] + landed[step, 0] + landed[step, 1]
        return 0.85 * arrived + 0.15

    smalls[3].wait()
    start = jnp.concatenate(
        [mass_ref[pl.ds(b * tile, tile)].reshape(1, tile) for b in range(blocks)], axis=0
    )

    def power(step, mass):
        raw = spread(step, mass)
        norm_begin(step, raw)
        return raw * norm_end(step)

    raw = spread(POWER - 1, lax.fori_loop(0, POWER - 1, power, start))
    norm_begin(POWER - 1, raw)
    raw_halo[1] = raw
    raw_right = remote(raw_halo.at[1], raw_halo.at[0], halo_send.at[0], halo_recv.at[0], right)
    raw_left = remote(raw_halo.at[1], raw_halo.at[2], halo_send.at[1], halo_recv.at[1], left)
    raw_right.start()
    raw_left.start()
    norm = norm_end(POWER - 1)
    root = jnp.sqrt(raw * norm)
    root_inverse = 1.0 / root
    gain = root * row_inverse

    halves = tile // 128
    for b in range(blocks):
        probe = probe_ref[:, b * tile : (b + 1) * tile].astype(F32)
        pushed = (probe * gain[b : b + 1]).astype(BF16)
        for k in range(slots):
            product = jnp.dot(pushed, tiles[b, k], preferred_element_type=F32)
            at = (b * slots + k) * chans
            for h in range(halves):
                products[h, at : at + chans, :] = product[:, h * 128 : (h + 1) * 128]
    part_copies = []
    for chunk in range(2):
        begin, end = chunk * chans // 2, (chunk + 1) * chans // 2
        for c in range(begin, end):
            slab = jnp.concatenate(
                [products.at[h][pl.ds(c, pairs, stride=chans), :] for h in range(halves)], axis=1
            )
            parts = jnp.concatenate(split3(slab), axis=0)
            placed = jnp.dot(place3, parts, preferred_element_type=F32)
            for h in range(halves):
                column = placed[:, h * 128 : (h + 1) * 128]
                low[h, c * blocks : (c + 1) * blocks, :] = column[:blocks]
                mid[h, c * blocks : (c + 1) * blocks, :] = column[blocks : 2 * blocks]
                up[h, c * blocks : (c + 1) * blocks, :] = column[2 * blocks : 3 * blocks]
        some = pl.ds(begin * blocks, (end - begin) * blocks)
        to_left = remote(
            low.at[:, some], from_right.at[:, some],
            part_send.at[0, chunk], part_recv.at[0, chunk], left,
        )
        to_right = remote(
            up.at[:, some], from_left.at[:, some],
            part_send.at[1, chunk], part_recv.at[1, chunk], right,
        )
        to_left.start()
        to_right.start()
        part_copies += [to_left, to_right]

    probe_right.wait_recv()
    probe_left.wait_recv()
    raw_right.wait_recv()
    raw_left.wait_recv()
    quads = 128 // chans
    pieces = []
    for side, part in ((0, 0), (1, None), (2, 1)):
        if part is None:
            inverse = root_inverse
        else:
            inverse = 1.0 / jnp.sqrt(raw_halo[side] * norm)
        for b in range(blocks):
            lanes = slice(b * tile, (b + 1) * tile)
            probe = probe_ref[:, lanes] if part is None else probe_halo[part, :, lanes]
            pieces.append(probe.astype(F32) * inverse[b : b + 1])
            if len(pieces) == quads:
                at = (side * blocks + b) // quads
                scaled[at] = jnp.concatenate(pieces, axis=0).T.astype(BF16)
                pieces = []
    quad_lane = lax.broadcasted_iota(jnp.int32, (16, 128), 1) // chans
    for b in range(blocks):
        sums_up = jnp.zeros((tile, 128), F32)
        for k in range(slots):
            at = spot[b * slots + k]
            pick = jnp.where(quad_lane == lax.rem(at, quads), 1.0, 0.0).astype(BF16)
            chosen = scaled[at // quads] * jnp.concatenate([pick] * (tile // 16), axis=0)
            sums_up += jnp.dot(tiles[b, k], chosen, preferred_element_type=F32)
        turned = sums_up.T
        forward = turned[:chans]
        for q in range(1, quads):
            forward += turned[q * chans : (q + 1) * chans]
        embedded[:, b * tile : (b + 1) * tile] = forward * gain[b : b + 1]

    for copy in part_copies:
        copy.wait_recv()
    for b in range(blocks):
        for h in range(halves):
            lanes = slice(b * tile + h * 128, b * tile + (h + 1) * 128)
            rows = pl.ds(b, chans, stride=blocks)
            arrived = mid.at[h][rows, :] + from_left.at[h][rows, :] + from_right.at[h][rows, :]
            back = arrived * root_inverse[b : b + 1, h * 128 : (h + 1) * 128]
            value = 0.5 * (embedded[:, lanes] + back)
            for index, piece in enumerate(split3(value)):
                emb_parts[index * chans : (index + 1) * chans, lanes] = piece

    cross = lax.dot_general(
        emb_parts[...], emb_parts[...], contract_last, preferred_element_type=F32
    )
    gram = jnp.zeros((chans, chans), F32)
    for i, j in ((2, 2), (1, 2), (2, 1), (0, 2), (2, 0), (1, 1), (0, 1), (1, 0), (0, 0)):
        gram += cross[i * chans : (i + 1) * chans, j * chans : (j + 1) * chans]
    quarters = chans // 8
    grams[me] = jnp.concatenate([gram[q * 8 : (q + 1) * 8] for q in range(quarters)], axis=1)
    each(
        devices,
        lambda offset: remote(
            grams.at[me], grams.at[me], gram_send, gram_recv, other(offset)
        ).start(),
    )
    wait_all(grams, gram_recv, devices)
    packed = jnp.sum(grams[...], axis=0)
    gram = jnp.concatenate(
        [packed[:, q * chans : (q + 1) * chans] for q in range(quarters)], axis=0
    )

    wide = (chans, 2 * chans)
    row_id = lax.broadcasted_iota(jnp.int32, (chans, chans), 0)
    col_id = lax.broadcasted_iota(jnp.int32, (chans, chans), 1)
    work = jnp.concatenate([gram, jnp.where(row_id == col_id, 1.0, 0.0)], axis=1)
    row_wide = lax.broadcasted_iota(jnp.int32, wide, 0)
    pivots = jnp.ones(wide, F32)
    panel = 4
    for k in range(0, chans, panel):
        rows = [jnp.broadcast_to(work[k + i : k + i + 1], wide) for i in range(panel)]
        columns = [
            jnp.broadcast_to(work[:, k + i : k + i + 1], wide) for i in range(panel)
        ]
        corner = [
            [jnp.broadcast_to(columns[j][k + i : k + i + 1], wide) for j in range(i + 1)]
            for i in range(panel)
        ]
        for j in range(panel):
            pivots = jnp.where(row_wide == k + j, corner[j][j], pivots)
            inverse_pivot = 1.0 / corner[j][j]
            factors = [corner[i][j] * inverse_pivot for i in range(j + 1, panel)]
            for i in range(j + 1, panel):
                factor = factors[i - j - 1]
                rows[i] = rows[i] - factor * rows[j]
                columns[i] = columns[i] - factor * columns[j]
                for m in range(j + 1, i + 1):
                    corner[i][m] = corner[i][m] - factor * corner[m][j]
            below = jnp.where(row_wide > k + j, columns[j], 0.0)
            work = work - below * (rows[j] * inverse_pivot)
    inverse = (work * lax.rsqrt(pivots))[:, chans:]
    ih, im, il = split3(inverse)
    lhs = jnp.concatenate([ih, im, il, ih, im, ih], axis=1)
    eh = emb_parts[:chans]
    em = emb_parts[chans : 2 * chans]
    el = emb_parts[2 * chans :]
    rhs = jnp.concatenate([eh, eh, eh, em, em, el], axis=0)
    out_ref[...] = jnp.dot(lhs, rhs, preferred_element_type=F32)

    probe_right.wait_send()
    probe_left.wait_send()
    raw_right.wait_send()
    raw_left.wait_send()
    for copy in part_copies:
        copy.wait_send()

    def drain(step, carry):
        wait_all(sums.at[step], sum_send.at[step], devices)
        for side, at in ((0, 0), (1, 2 * blocks)):
            view = window.at[step, pl.ds(at, blocks)]
            pltpu.make_async_copy(view, view, win_send.at[step, side]).wait()
        return carry

    lax.fori_loop(0, POWER, drain, 0)
    wait_all(grams, gram_send, devices)


def per_device(row_axis, col_axis, tile_blocks, tile_cols, tile_count, start_mass, probe_block):
    blocks, slots, tile = tile_blocks.shape[:3]
    chans = probe_block.shape[0]
    devices = row_axis * col_axis
    zones = blocks * tile
    halves = tile // 128
    vmem = pl.BlockSpec(memory_space=pltpu.VMEM)
    in_hbm = pl.BlockSpec(memory_space=pltpu.HBM)
    dma = pltpu.SemaphoreType.DMA
    part = pltpu.VMEM((halves, chans * blocks, 128), F32)
    return pl.pallas_call(
        functools.partial(kernel, row_axis, col_axis, blocks, slots, tile, chans),
        out_shape=jax.ShapeDtypeStruct((chans, zones), F32),
        in_specs=[in_hbm] * 5,
        out_specs=vmem,
        scratch_shapes=[
            pltpu.SMEM(tile_cols.shape, jnp.int32),
            pltpu.SMEM(tile_count.shape, jnp.int32),
            pltpu.VMEM(start_mass.shape, F32),
            pltpu.VMEM(probe_block.shape, BF16),
            pltpu.VMEM((blocks, slots, tile, tile), BF16),
            pltpu.VMEM((blocks, 4 * blocks, slots * tile), BF16),
            pltpu.VMEM((POWER, 3 * blocks, tile), F32),
            pltpu.VMEM((POWER, 2, blocks, tile), F32),
            pltpu.VMEM((3, blocks, tile), F32),
            pltpu.VMEM((POWER, devices, 1, 128), F32),
            pltpu.VMEM((2, chans, zones), BF16),
            pltpu.VMEM((3 * blocks * chans // 128 + 1, tile, 128), BF16),
            pltpu.VMEM((halves, blocks * slots * chans, 128), F32),
            part, part, part, part, part,
            pltpu.VMEM((3 * chans, zones), BF16),
            pltpu.VMEM((chans, zones), F32),
            pltpu.VMEM((devices, 8, 128), F32),
            dma((4,)),
            dma((blocks,)),
            dma((POWER,)), dma((POWER,)),
            dma((POWER, 2)), dma((POWER, 2)),
            dma((2,)), dma((2,)),
            dma((2,)), dma((2,)),
            dma((2, 2)), dma((2, 2)),
            dma, dma,
        ],
        compiler_params=pltpu.CompilerParams(
            collective_id=0, has_side_effects=True, vmem_limit_bytes=64 * 1024 * 1024
        ),
        name="embed",
    )(tile_cols, tile_count, tile_blocks, start_mass, probe_block)


def solution(mesh):
    sizes = dict(mesh.shape)
    return jax.shard_map(
        functools.partial(per_device, sizes["rows"], sizes["cols"]),
        mesh=mesh,
        in_specs=(
            P(("rows", "cols"), None, None, None),
            P(("rows", "cols"), None),
            P(("rows", "cols")),
            P(("rows", "cols")),
            P(None, ("rows", "cols")),
        ),
        out_specs=P(None, ("rows", "cols")),
        check_vma=False,
    )
```
